128 devices in a mesh: prow: 8 (over x_lo, z), pcol: 16 (over x_hi, y, core).
Axes of the slice: x: 4 (x_hi: 2, x_lo: 2; x = x_hi * 2 + x_lo), y: 4, z: 4, core: 2. Of those that a mesh axis runs over, the one named last changes fastest.
Arguments:
- k_star: float32 [4, 16, 512, 256], P(None, 'pcol', 'prow'), may hold values from -6 to 6
- lower_blocks: float32 [6, 16, 512, 8192], P(None, None, 'prow', 'pcol'), may hold values from -0.046875 to 0.046875
- diag_inverse: float32 [4, 16, 512, 8192], P(None, None, 'prow', 'pcol'), may hold values from -1 to 2, as said below
Outputs:
- forward_solution: float32 [4, 16, 512, 256], P(None, 'pcol', 'prow')
- solution: float32 [4, 16, 512, 256], P(None, 'pcol', 'prow')
The draws below stay inside these ranges and needn't reach their ends.
Inputs may be any that keep to these rules, and one draw needn't show every extreme that they name: Each of the 4 blocks of diag_inverse is lower triangular with a positive diagonal.
All inputs are finite; a program needn't handle non-finite values.
Results may differ from the reference program's by a relative error of at most 0.00013.
Values sent between devices are 32-bit elements; how exact they have to be, the bound alone decides.
A program may use at most 128 MiB of HBM per device.

```python
import math
import jax
import jax.numpy as jnp
from jax import lax

BR = 8192
STEPS = 4
NRHS = 256
PAIRS = 6
N_PCOL = 16


def draw_diag_inverse(key, part):
    key = jax.random.fold_in(key, 11)
    first, second = jax.random.split(key)
    shape = (STEPS, N_PCOL, BR // N_PCOL, BR)
    rows = lax.broadcasted_iota(jnp.int32, shape, 1) * (BR // N_PCOL) + lax.broadcasted_iota(jnp.int32, shape, 2)
    cols = lax.broadcasted_iota(jnp.int32, shape, 3)
    spread = jax.random.normal(first, shape, jnp.float32)
    diag = jnp.exp(jax.random.uniform(second, shape, jnp.float32, math.log(0.5), math.log(2.0)))
    below = jnp.where(cols < rows, spread * (1.0 / math.sqrt(BR)), 0.0)
    return jnp.where(cols == rows, diag, below)


def levels(stream_key, extent, cuts, least, high):
    def one(dim, shards_of):
        steps = jax.random.uniform(jax.random.fold_in(jax.random.fold_in(stream_key, 6), dim), (shards_of,), jnp.float32, least / len(cuts), high / len(cuts))
        return jnp.repeat(jnp.exp(steps), extent[dim] // shards_of).reshape((-1,) + (1,) * (len(extent) - dim - 1))

    factor_of = one(*cuts[0])
    for cut in cuts[1:]:
        factor_of = factor_of * one(*cut)
    return factor_of


def gaussian(key, dims, scale, most, shards=(), dtype=jnp.bfloat16):
    values = jax.random.normal(key, dims, jnp.float32) * scale
    if len(shards) > 0:
        values = levels(key, dims, shards, -0.22, 0.18) * values
    return jnp.clip(values, min=-most, max=most).astype(dtype)


def setup_inputs(seed: int = 0) -> dict:
    key_list = jax.random.split(jax.random.key(seed), 4)
    return {
        "k_star": gaussian(key_list[0], (STEPS, N_PCOL, BR // N_PCOL, NRHS), 1.0, 6.0, ((1, 16), (2, 8)), jnp.float32),
        "lower_blocks": gaussian(key_list[1], (PAIRS, N_PCOL, BR // N_PCOL, BR), (2 * BR) ** -0.5, 0.046875, ((2, 8), (3, 16)), jnp.float32),
        "diag_inverse": draw_diag_inverse(jax.random.fold_in(key_list[3], 71), 0),
    }


def product(left, right):
    return jnp.dot(left, right, precision=lax.Precision.HIGHEST, preferred_element_type=jnp.float32)


def product_left(left, right):
    return lax.dot_general(left, right, (((0,), (0,)), ((), ())), precision=lax.Precision.HIGHEST, preferred_element_type=jnp.float32)


def reference(k_star, lower_blocks, diag_inverse):
    rhs = k_star.reshape(STEPS, BR, NRHS)
    lower = lower_blocks.reshape(PAIRS, BR, BR)
    inverse = diag_inverse.reshape(STEPS, BR, BR)
    forward = []
    for block in range(STEPS):
        reduced = rhs[block]
        for other in range(block):
            reduced = reduced - product(lower[block * (block - 1) // 2 + other], forward[other])
        forward.append(product(inverse[block], reduced))
    backward = [None] * STEPS
    for block in range(STEPS - 1, -1, -1):
        reduced = forward[block]
        for other in range(block + 1, STEPS):
            reduced = reduced - product_left(lower[other * (other - 1) // 2 + block], backward[other])
        backward[block] = product_left(inverse[block], reduced)
    shape = (STEPS, N_PCOL, BR // N_PCOL, NRHS)
    return jnp.stack(forward).reshape(shape), jnp.stack(backward).reshape(shape)
```

```python
import jax
import jax.numpy as jnp
from jax import lax
from jax.experimental import pallas as pl
from jax.experimental.pallas import tpu as pltpu
from jax.sharding import PartitionSpec as P

MESH = pl.DeviceIdType.MESH
F32 = jnp.float32
BF16 = jnp.bfloat16

SLOTS = 4
TILES = [
    ("E", 0), ("L", 1, 0), ("L", 2, 0), ("L", 3, 0), ("E", 1),
    ("L", 2, 1), ("L", 3, 1), ("E", 2), ("L", 3, 2), ("E", 3),
]
TILE = {name: index for index, name in enumerate(TILES)}


def dot(a, b):
    return lax.dot_general(a, b, (((1,), (0,)), ((), ())), preferred_element_type=F32)


def dot_t(a, b):
    return lax.dot_general(a, b, (((0,), (0,)), ((), ())), preferred_element_type=F32)


def split(value):
    high = value.astype(BF16)
    return high, (value - high.astype(F32)).astype(BF16)


def kernel(
    k_ref, l_ref, e_ref, y_ref, x_ref,
    stage, mh, ml, u, v, cbuf, rbuf, g, bh, bl, facc,
    gb, ch_, cl_, w, wbuf, bacc,
    ld_sem, core_s, core_r, rs_s, rs_r, ag_s, ag_r,
    bag_s, bag_r, rel_s, rel_r, brs_s, brs_r,
):
    r = lax.axis_index("prow")
    p = lax.axis_index("pcol")
    c = lax.rem(p, 2)
    q = p // 2
    mate = (r, p + 1 - 2 * c)

    def peer(other):
        return (r, 2 * other + c)

    def turn(base, step, n):
        return lax.rem(base + step, n)

    def load(i, rel):
        name = TILES[i]
        s = i % SLOTS
        half = 1 - c if rel == 0 else c
        if name[0] == "E":
            src = e_ref.at[name[1], :, half]
        else:
            src = l_ref.at[name[1] * (name[1] - 1) // 2 + name[2], :, half]
        return pltpu.make_async_copy(src, stage.at[s, rel], ld_sem.at[s, rel])

    def convert(i):
        s = i % SLOTS
        for rel in range(2):
            load(i, rel).wait()

            @pl.loop(0, 8)
            def _(a):
                high, low = split(stage[s, rel, a])
                rows = pl.ds(pl.multiple_of(a * 64, 64), 64)
                mh[i, rel, rows, :] = high
                ml[i, rel, rows, :] = low

        if i + SLOTS < len(TILES):
            for rel in range(2):
                load(i + SLOTS, rel).start()

    for i in range(SLOTS):
        for rel in range(2):
            load(i, rel).start()

    barrier = pltpu.get_barrier_semaphore()
    pl.semaphore_signal(barrier, inc=1, device_id=mate, device_id_type=MESH)
    for j in range(1, 8):
        pl.semaphore_signal(barrier, inc=1, device_id=peer(turn(q, j, 8)), device_id_type=MESH)
        pl.semaphore_signal(barrier, inc=1, device_id=(turn(r, j, 8), p), device_id_type=MESH)
    pl.semaphore_wait(barrier, 15)

    def remote(src, dst, send, recv, device):
        return pltpu.make_async_remote_copy(
            src_ref=src, dst_ref=dst, send_sem=send, recv_sem=recv, device_id=device, device_id_type=MESH
        )

    def gemm(i, rel, rows, b):
        ah, al = mh[i, rel, rows, :], ml[i, rel, rows, :]
        return dot(ah, bh[b]) + dot(ah, bl[b]) + dot(al, bh[b])

    def pair_rows(pair):
        return pl.ds(pl.multiple_of(pair * 128, 128), 128)

    def fwd_filler(i, b, slot, first):
        def run():
            for rel in range(2):

                @pl.loop(0, 4)
                def _(pair):
                    rows = pair_rows(pair)
                    out = gemm(i, rel, rows, b)
                    facc[slot, rel, rows, :] = out if first else facc[slot, rel, rows, :] + out

        return run

    def fwd_rs(t, i, b, slot, fillers):
        par = t % 2
        home = q // 2

        def core(pair, j):
            rows = pair_rows(pair)
            return remote(u.at[par, rows], cbuf.at[par, rows], core_s.at[par, j], core_r.at[par, j], mate)

        pairs = [turn(home, j, 4) for j in (1, 2, 3, 0)]
        for j, pair in enumerate(pairs):
            rows = pair_rows(pair)
            out = gemm(i, 0, rows, b)
            u[par, rows, :] = out if slot is None else out + facc[slot, 0, rows, :]
            core(pair, j).start()
        for j, pair in enumerate(pairs):
            rows = pair_rows(pair)
            out = gemm(i, 1, rows, b)
            v[par, rows, :] = out if slot is None else out + facc[slot, 1, rows, :]

        def message(other):
            rows = pl.ds(pl.multiple_of(other * 64, 64), 64)
            return remote(
                v.at[par, rows], rbuf.at[par, q], rs_s.at[par, other], rs_r.at[par, q], peer(other)
            )

        for j, pair in enumerate(pairs):
            rows = pair_rows(pair)
            core(pair, j).wait_recv()
            v[par, rows, :] = v[par, rows, :] + cbuf[par, rows, :]
            if j < 3:
                message(2 * pair).start()
                message(2 * pair + 1).start()
            else:
                message(q + 1 - 2 * lax.rem(q, 2)).start()
        for run in fillers:
            run()
        total = v[par, pl.ds(pl.multiple_of(q * 64, 64), 64), :]
        for j in range(1, 8):
            s = turn(q, j, 8)
            remote(rbuf.at[par, s], rbuf.at[par, s], rs_s.at[par, s], rs_r.at[par, s], mate).wait_recv()
            total = total + rbuf[par, s]
        for j, pair in enumerate(pairs):
            core(pair, j).wait_send()
        for j in range(1, 8):
            message(turn(q, j, 8)).wait_send()
        return total

    def fwd_ag(t, value, b, fillers):
        par = t % 2
        g[t, r] = value

        def message(j):
            return remote(
                g.at[t, r], g.at[t, r], ag_s.at[par, j], ag_r.at[par, r], (turn(r, j, 8), p)
            )

        for j in range(1, 8):
            message(j).start()
        for run in fillers:
            run()
        for j in range(8):
            s = turn(r, j, 8)
            if j > 0:
                remote(g.at[t, s], g.at[t, s], ag_s.at[par, j], ag_r.at[par, s], mate).wait_recv()
            rows = pl.ds(pl.multiple_of(s * 64, 64), 64)
            high, low = split(g[t, s])
            bh[b, rows, :] = high
            bl[b, rows, :] = low
        for j in range(1, 8):
            message(j).wait_send()

    def conv(*names):
        return [lambda i=TILE[name]: convert(i) for name in names]

    fwd_ag(0, k_ref[0], 0, conv(("E", 0), ("L", 1, 0)))
    late = {0: conv(("L", 2, 0), ("L", 3, 0)), 1: conv(("L", 3, 1),), 2: conv(("E", 3)), 3: []}
    fill_rs = {
        0: [fwd_filler(TILE["L", 2, 0], 1, 0, True)],
        1: [fwd_filler(TILE["L", 3, 1], 1, 1, False)],
        2: [],
    }
    fill_ag = {
        0: [fwd_filler(TILE["L", 3, 0], 1, 1, True)] + conv(("E", 1), ("L", 2, 1)),
        1: conv(("E", 2), ("L", 3, 2)),
        2: [],
    }
    for k in range(4):
        y_ref[k] = fwd_rs(2 * k, TILE["E", k], 0, None, late[k])
        if k < 3:
            fwd_ag(2 * k + 1, y_ref[k], 1, [])
            slot = None if k == 0 else k - 1
            down = fwd_rs(2 * k + 1, TILE["L", k + 1, k], 1, slot, fill_rs[k])
            fwd_ag(2 * k + 2, k_ref[k + 1] - down, 0, fill_ag[k])

    def gemm_t(i, rel, cols, b):
        ah, al = mh[i, rel, :, cols], ml[i, rel, :, cols]
        return dot_t(ah, ch_[b, rel]) + dot_t(ah, cl_[b, rel]) + dot_t(al, ch_[b, rel])

    def bwd_ag(t, value, b, fillers):
        par = t % 2
        gb[t, 1, q] = value

        def message(j):
            return remote(
                gb.at[t, 1, q], gb.at[t, 1, q], bag_s.at[par, j], bag_r.at[par, q], peer(turn(q, j, 8))
            )

        def relay(s):
            return remote(gb.at[t, 1, s], gb.at[t, 0, s], rel_s.at[par, s], rel_r.at[par, s], mate)

        def take(rel, s):
            rows = pl.ds(pl.multiple_of(s * 64, 64), 64)
            high, low = split(gb[t, rel, s])
            ch_[b, rel, rows, :] = high
            cl_[b, rel, rows, :] = low

        for j in range(1, 8):
            message(j).start()
        relay(q).start()
        for run in fillers:
            run()
        for j in range(8):
            s = turn(q, j, 8)
            if j > 0:
                remote(gb.at[t, 1, s], gb.at[t, 1, s], bag_s.at[par, j], bag_r.at[par, s], mate).wait_recv()
                relay(s).start()
            take(1, s)
        for j in range(8):
            s = turn(q, j, 8)
            relay(s).wait_recv()
            take(0, s)
        for j in range(1, 8):
            message(j).wait_send()
        for j in range(8):
            relay(turn(q, j, 8)).wait_send()

    def bwd_filler(i, b, slot, first):
        def run():
            for pair in range(4):
                cols = pl.ds(pair * 128, 128)
                out = gemm_t(i, 0, cols, b) + gemm_t(i, 1, cols, b)
                bacc[slot, cols, :] = out if first else bacc[slot, cols, :] + out

        return run

    def bwd_rs(t, i, b, slot, fillers):
        par = t % 2

        def message(j):
            other = turn(r, j, 8)
            rows = pl.ds(pl.multiple_of(other * 64, 64), 64)
            return remote(
                w.at[par, rows], wbuf.at[par, r], brs_s.at[par, j], brs_r.at[par, r], (other, p)
            )

        for pair in range(4):
            cols = pl.ds(pair * 128, 128)
            out = gemm_t(i, 0, cols, b) + gemm_t(i, 1, cols, b)
            w[par, cols, :] = out if slot is None else out + bacc[slot, cols, :]
        for j in range(1, 8):
            message(j).start()
        for run in fillers:
            run()
        total = w[par, pl.ds(pl.multiple_of(r * 64, 64), 64), :]
        for j in range(1, 8):
            s = turn(r, j, 8)
            remote(wbuf.at[par, s], wbuf.at[par, s], brs_s.at[par, j], brs_r.at[par, s], mate).wait_recv()
            total = total + wbuf[par, s]
        for j in range(1, 8):
            message(j).wait_send()
        return total

    back_rs = {
        3: [bwd_filler(TILE["L", 3, 1], 1, 1, True)],
        2: [bwd_filler(TILE["L", 2, 0], 1, 0, False)],
        1: [],
    }
    back_ag = {3: [bwd_filler(TILE["L", 3, 0], 1, 0, True)], 2: [], 1: []}
    t = 0
    bwd_ag(0, y_ref[3], 0, [])
    for k in range(3, -1, -1):
        x_ref[k] = bwd_rs(t, TILE["E", k], 0, None, [])
        if k > 0:
            bwd_ag(t + 1, x_ref[k], 1, [])
            slot = None if k == 3 else k - 1
            up = bwd_rs(t + 1, TILE["L", k, k - 1], 1, slot, back_rs[k])
            bwd_ag(t + 2, y_ref[k - 1] - up, 0, back_ag[k])
            t += 2


def local(k_star, lower_blocks, diag_inverse):
    steps, _, piece, cols = k_star.shape
    pairs, groups, _, width = lower_blocks.shape
    dma = pltpu.SemaphoreType.DMA
    n = len(TILES)
    y, x = pl.pallas_call(
        kernel,
        out_shape=[jax.ShapeDtypeStruct((steps, piece, cols), F32)] * 2,
        in_specs=[
            pl.BlockSpec(memory_space=pltpu.VMEM),
            pl.BlockSpec(memory_space=pl.ANY),
            pl.BlockSpec(memory_space=pl.ANY),
        ],
        out_specs=[pl.BlockSpec(memory_space=pltpu.VMEM)] * 2,
        scratch_shapes=[
            pltpu.VMEM((SLOTS, 2, 8, 64, 512), F32),
            pltpu.VMEM((n, 2, 512, 512), BF16),
            pltpu.VMEM((n, 2, 512, 512), BF16),
            pltpu.VMEM((2, 512, 256), F32),
            pltpu.VMEM((2, 512, 256), F32),
            pltpu.VMEM((2, 512, 256), F32),
            pltpu.VMEM((2, 8, 64, 256), F32),
            pltpu.VMEM((7, 8, 64, 256), F32),
            pltpu.VMEM((2, 512, 256), BF16),
            pltpu.VMEM((2, 512, 256), BF16),
            pltpu.VMEM((2, 2, 512, 256), F32),
            pltpu.VMEM((7, 2, 8, 64, 256), F32),
            pltpu.VMEM((2, 2, 512, 256), BF16),
            pltpu.VMEM((2, 2, 512, 256), BF16),
            pltpu.VMEM((2, 512, 256), F32),
            pltpu.VMEM((2, 8, 64, 256), F32),
            pltpu.VMEM((2, 512, 256), F32),
            dma((SLOTS, 2)),
            dma((2, 4)), dma((2, 4)),
            dma((2, 8)), dma((2, 8)),
            dma((2, 8)), dma((2, 8)),
            dma((2, 8)), dma((2, 8)),
            dma((2, 8)), dma((2, 8)),
            dma((2, 8)), dma((2, 8)),
        ],
        compiler_params=pltpu.CompilerParams(
            collective_id=0, has_side_effects=True, vmem_limit_bytes=60 * 1024 * 1024
        ),
    )(
        k_star.reshape(steps, piece, cols),
        lower_blocks.reshape(pairs, groups // 2, 2, piece, width),
        diag_inverse.reshape(steps, groups // 2, 2, piece, width),
    )
    shape = (steps, 1, piece, cols)
    return y.reshape(shape), x.reshape(shape)


def solution(mesh):
    return jax.shard_map(
        local,
        mesh=mesh,
        in_specs=(
            P(None, "pcol", "prow", None),
            P(None, None, "prow", "pcol"),
            P(None, None, "prow", "pcol"),
        ),
        out_specs=(P(None, "pcol", "prow", None), P(None, "pcol", "prow", None)),
        check_vma=False,
    )
```

```python
import jax
import jax.numpy as jnp
from jax import lax
from jax.experimental import pallas as pl
from jax.experimental.pallas import tpu as pltpu
from jax.sharding import PartitionSpec as P

MESH = pl.DeviceIdType.MESH
F32 = jnp.float32
BF16 = jnp.bfloat16

SLOTS = 4
CHUNK = 256
TILES = [
    ("E", 0), ("L", 1, 0), ("E", 1), ("L", 2, 1), ("L", 2, 0),
    ("L", 3, 0), ("E", 2), ("L", 3, 2), ("L", 3, 1), ("E", 3),
]
TILE = {name: index for index, name in enumerate(TILES)}
HALVES = 2 * len(TILES)
FAR_FIRST = [(1, 2), (1, 1), (1, 3), (0, 2), (1, 0), (0, 1), (0, 3)]


def dot(a, b):
    return lax.dot_general(a, b, (((1,), (0,)), ((), ())), preferred_element_type=F32)


def dot_t(a, b):
    return lax.dot_general(a, b, (((0,), (0,)), ((), ())), preferred_element_type=F32)


def split(value):
    high = value.astype(BF16)
    return high, (value - high.astype(F32)).astype(BF16)


def kernel(
    k_ref, l_ref, e_ref, y_ref, x_ref,
    stage, mh, ml, part, acc, ops, gf, gb, rf, rb, ksend, krecv, kx, yfull, xfull, ybuf, xbuf,
    ld_sem, mate_s, mate_r, free, io_s, io_r,
    rs_s, rs_r, ag_s, ag_r, brs_s, brs_r, bag_s, bag_r,
):
    r = lax.axis_index("prow")
    p = lax.axis_index("pcol")
    c = lax.rem(p, 2)
    q = p // 2
    mate = (r, p + 1 - 2 * c)

    def member(me, offset):
        return lax.rem(me // 4 + offset[0], 2) * 4 + lax.rem(lax.rem(me, 4) + offset[1], 4)

    def on_q(offset):
        return (r, 2 * member(q, offset) + c)

    def on_r(offset):
        return (member(r, offset), p)

    def remote(src, dst, send, recv, device):
        return pltpu.make_async_remote_copy(
            src_ref=src, dst_ref=dst, send_sem=send, recv_sem=recv, device_id=device, device_id_type=MESH
        )

    def source(n):
        name, half = TILES[n // 2], n % 2
        if name[0] == "E":
            return e_ref.at[name[1], :, half]
        return l_ref.at[name[1] * (name[1] - 1) // 2 + name[2], :, half]

    def own(n):
        s = n % SLOTS
        return pltpu.make_async_copy(source(n), stage.at[s, c], ld_sem.at[s])

    def shared(n):
        s = n % SLOTS
        return remote(source(n), stage.at[s, c], mate_s.at[s], mate_r.at[s], mate)

    def convert(n):
        s = n % SLOTS
        own(n).wait()
        shared(n).wait()
        for kh in range(2):

            @pl.loop(0, 8)
            def _(a):
                high, low = split(stage[s, kh, a])
                rows = pl.ds(pl.multiple_of(a * 64, 64), 64)
                mh[n // 2, kh, n % 2, rows, :] = high
                ml[n // 2, kh, n % 2, rows, :] = low

        if n + SLOTS < HALVES:
            pl.semaphore_signal(free, inc=1, device_id=mate, device_id_type=MESH)
        following = n - 1 + SLOTS
        if n >= 1 and following < HALVES:
            pl.semaphore_wait(free, 1)
            own(following).start()
            shared(following).start()

    for n in range(SLOTS):
        own(n).start()
    for k in range(4):
        left, right = k_ref[k, :, 0:128], k_ref[k, :, 128:256]
        kx[k, c] = jnp.where(c == 0, left, right)
        ksend[k] = jnp.where(c == 0, right, left)

    barrier = pltpu.get_barrier_semaphore()
    pl.semaphore_signal(barrier, inc=1, device_id=mate, device_id_type=MESH)
    for offset in FAR_FIRST:
        pl.semaphore_signal(barrier, inc=1, device_id=on_q(offset), device_id_type=MESH)
        pl.semaphore_signal(barrier, inc=1, device_id=on_r(offset), device_id_type=MESH)
    pl.semaphore_wait(barrier, 15)

    columns = remote(ksend, krecv, io_s.at[8], io_r.at[8], mate)
    columns.start()
    for n in range(SLOTS):
        shared(n).start()
    columns.wait()
    for k in range(4):
        kx[k, 1 - c] = krecv[k]

    class Forward:
        g, rbuf, me, sum_me = gf, rf, r, q
        ag, rs = (ag_s, ag_r), (rs_s, rs_r)
        on_ag, on_rs = staticmethod(on_r), staticmethod(on_q)

        @staticmethod
        def product(i, kh, oh, b, at):
            rows = pl.ds(at, CHUNK)
            wide = dot(mh[i, kh, oh, rows, :], ops[b, kh])
            return wide[:, 0:128] + wide[:, 128:256] + dot(ml[i, kh, oh, rows, :], ops[b, kh, :, 0:128])

    class Backward:
        g, rbuf, me, sum_me = gb, rb, q, r
        ag, rs = (bag_s, bag_r), (brs_s, brs_r)
        on_ag, on_rs = staticmethod(on_q), staticmethod(on_r)

        @staticmethod
        def product(i, kh, oh, b, at):
            cols = pl.ds(at, CHUNK)
            wide = dot_t(mh[i, oh, kh, :, cols], ops[b, kh])
            return wide[:, 0:128] + wide[:, 128:256] + dot_t(ml[i, oh, kh, :, cols], ops[b, kh, :, 0:128])

    PER = CHUNK // 64

    def chunks():
        return range(0, 512, CHUNK)

    def groups(value):
        return value.reshape(PER, 64, 128)

    def gather_start(way, par, h, value):
        way.g[par, h, way.me] = value
        for offset in FAR_FIRST:
            remote(
                way.g.at[par, h, way.me], way.g.at[par, h, way.me],
                way.ag[0].at[par, h], way.ag[1].at[par, h], way.on_ag(offset),
            ).start()

    def seven(buf, sems, par, h):
        view = buf.at[par, h, pl.ds(0, 7)]
        return remote(view, view, sems[0].at[par, h], sems[1].at[par, h], mate)

    def gather_finish(way, par, h, b):
        seven(way.g, way.ag, par, h).wait_recv()
        high, low = split(way.g[par, h].reshape(512, 128))
        ops[b, h, :, 0:128] = high
        ops[b, h, :, 128:256] = low

    def sum_start(way, par, h):
        for j, offset in enumerate(FAR_FIRST):
            remote(
                part.at[par, h, member(way.sum_me, offset)], way.rbuf.at[par, h, j],
                way.rs[0].at[par, h], way.rs[1].at[par, h], way.on_rs(offset),
            ).start()

    def sum_finish(way, par, h):
        total = part[par, h, way.sum_me]
        seven(way.rbuf, way.rs, par, h).wait_recv()
        for j in range(7):
            total = total + way.rbuf[par, h, j]
        return total

    def aside(way, i, b, slot, first):
        def run(oh):
            for at in chunks():
                out = way.product(i, 0, oh, b, at) + way.product(i, 1, oh, b, at)
                where = pl.ds(at // 64, PER)
                out = groups(out)
                acc[slot, oh, where] = out if first else acc[slot, oh, where] + out

        return [lambda oh=oh: run(oh) for oh in range(2)]

    def step(way, t, i, b, slot, after, summing, gathering):
        par = t % 2
        gather_finish(way, par, 0, b)
        for oh in range(2):
            for at in chunks():
                where = pl.ds(at // 64, PER)
                out = groups(way.product(i, 0, oh, b, at))
                part[par, oh, where] = out if slot is None else out + acc[slot, oh, where]
        gather_finish(way, par, 1, b)
        for oh in range(2):
            for at in chunks():
                where = pl.ds(at // 64, PER)
                part[par, oh, where] = part[par, oh, where] + groups(way.product(i, 1, oh, b, at))
            sum_start(way, par, oh)
        for h in range(2):
            seven(way.g, way.ag, par, h).wait_send()
        for run in summing:
            run()
        for h in range(2):
            after(h, sum_finish(way, par, h))
        for run in gathering:
            run()
        for h in range(2):
            seven(way.rbuf, way.rs, par, h).wait_send()

    def hand_over(full, buf, k, sem):
        return remote(full.at[k, 1 - c], buf.at[k], io_s.at[sem], io_r.at[sem], mate)

    def conv(*names):
        return [lambda n=n: convert(n) for name in names for n in (2 * TILE[name], 2 * TILE[name] + 1)]

    for h in range(2):
        gather_start(Forward, 0, h, kx[0, h])
    for run in conv(("E", 0)):
        run()
    fill = {
        ("E", 0): (conv(("L", 1, 0)), conv(("E", 1))),
        ("L", 0): (conv(("L", 2, 1)), conv(("L", 2, 0))),
        ("E", 1): (aside(Forward, TILE["L", 2, 0], 1, 0, True), conv(("L", 3, 0))),
        ("L", 1): (conv(("E", 2)), aside(Forward, TILE["L", 3, 0], 1, 1, True) + conv(("L", 3, 2))),
        ("E", 2): (conv(("L", 3, 1)), aside(Forward, TILE["L", 3, 1], 2, 1, False)),
        ("L", 2): (conv(("E", 3)), []),
        ("E", 3): ([], []),
    }
    for k in range(4):
        last = k == 3

        def solved(h, value, k=k, last=last):
            yfull[k, h] = value
            if last:
                gather_start(Backward, 0, h, value)
            else:
                gather_start(Forward, (2 * k + 1) % 2, h, value)

        step(Forward, 2 * k, TILE["E", k], 0, None, solved, *fill["E", k])
        hand_over(yfull, ybuf, k, k).start()
        if not last:

            def reduced(h, value, k=k):
                gather_start(Forward, (2 * k + 2) % 2, h, kx[k + 1, h] - value)

            slot = None if k == 0 else k - 1
            step(Forward, 2 * k + 1, TILE["L", k + 1, k], 1 + k, slot, reduced, *fill["L", k])

    fill = {
        ("E", 3): ([], []),
        ("L", 3): (aside(Backward, TILE["L", 3, 1], 1, 1, True), aside(Backward, TILE["L", 3, 0], 1, 0, True)),
        ("E", 2): ([], []),
        ("L", 2): (aside(Backward, TILE["L", 2, 0], 2, 0, False), []),
        ("E", 1): ([], []),
        ("L", 1): ([], []),
        ("E", 0): ([], []),
    }
    t = 0
    for k in range(3, -1, -1):

        def solved(h, value, k=k, t=t):
            xfull[k, h] = value
            if k > 0:
                gather_start(Backward, (t + 1) % 2, h, value)

        step(Backward, t, TILE["E", k], 0, None, solved, *fill["E", k])
        hand_over(xfull, xbuf, k, 4 + k).start()
        if k > 0:

            def reduced(h, value, k=k, t=t):
                gather_start(Backward, (t + 2) % 2, h, yfull[k - 1, h] - value)

            slot = None if k == 3 else k - 1
            step(Backward, t + 1, TILE["L", k, k - 1], 4 - k, slot, reduced, *fill["L", k])
            t += 2

    for k in range(4):
        hand_over(yfull, ybuf, k, k).wait()
        y_ref[k, c] = yfull[k, c]
        y_ref[k, 1 - c] = ybuf[k]
    for k in range(3, -1, -1):
        hand_over(xfull, xbuf, k, 4 + k).wait()
        x_ref[k, c] = xfull[k, c]
        x_ref[k, 1 - c] = xbuf[k]


def local(k_star, lower_blocks, diag_inverse):
    steps, _, piece, cols = k_star.shape
    pairs, segments, _, width = lower_blocks.shape
    dma = pltpu.SemaphoreType.DMA
    n = len(TILES)
    pieces = pltpu.VMEM((steps, 2, piece, cols // 2), F32)
    half = pltpu.VMEM((steps, piece, cols // 2), F32)
    slots = pltpu.VMEM((2, 2, 8, piece, cols // 2), F32)
    y, x = pl.pallas_call(
        kernel,
        out_shape=[jax.ShapeDtypeStruct((steps, 2, piece, cols // 2), F32)] * 2,
        in_specs=[
            pl.BlockSpec(memory_space=pltpu.VMEM),
            pl.BlockSpec(memory_space=pl.ANY),
            pl.BlockSpec(memory_space=pl.ANY),
        ],
        out_specs=[pl.BlockSpec(memory_space=pltpu.VMEM)] * 2,
        scratch_shapes=[
            pltpu.VMEM((SLOTS, 2, 8, piece, width), F32),
            pltpu.VMEM((n, 2, 2, 512, width), BF16),
            pltpu.VMEM((n, 2, 2, 512, width), BF16),
            slots,
            slots,
            pltpu.VMEM((4, 2, 512, 256), BF16),
            slots, slots,
            slots, slots,
            half, half,
            pieces, pieces, pieces,
            half, half,
            dma((SLOTS,)), dma((SLOTS,)), dma((SLOTS,)),
            pltpu.SemaphoreType.REGULAR,
            dma((9,)), dma((9,)),
            dma((2, 2)), dma((2, 2)),
            dma((2, 2)), dma((2, 2)),
            dma((2, 2)), dma((2, 2)),
            dma((2, 2)), dma((2, 2)),
        ],
        compiler_params=pltpu.CompilerParams(
            collective_id=0, has_side_effects=True, vmem_limit_bytes=62 * 1024 * 1024
        ),
    )(
        k_star.reshape(steps, piece, cols),
        lower_blocks.reshape(pairs, segments // 2, 2, piece, width),
        diag_inverse.reshape(steps, segments // 2, 2, piece, width),
    )

    def whole(value):
        return value.transpose(0, 2, 1, 3).reshape(steps, 1, piece, cols)

    return whole(y), whole(x)


def solution(mesh):
    return jax.shard_map(
        local,
        mesh=mesh,
        in_specs=(
            P(None, "pcol", "prow", None),
            P(None, None, "prow", "pcol"),
            P(None, None, "prow", "pcol"),
        ),
        out_specs=(P(None, "pcol", "prow", None), P(None, "pcol", "prow", None)),
        check_vma=False,
    )
```

```python
import jax
import jax.numpy as jnp
from jax import lax
from jax.experimental import pallas as pl
from jax.experimental.pallas import tpu as pltpu
from jax.sharding import PartitionSpec as P

MESH = pl.DeviceIdType.MESH
F32 = jnp.float32
BF16 = jnp.bfloat16

SLOTS = 4
CHUNK = 256
TILES = [
    ("E", 0), ("L", 1, 0), ("E", 1), ("L", 2, 1), ("L", 2, 0),
    ("L", 3, 0), ("E", 2), ("L", 3, 2), ("L", 3, 1), ("E", 3),
]
TILE = {name: index for index, name in enumerate(TILES)}
HALVES = 2 * len(TILES)
FAR_FIRST = [(1, 2), (1, 1), (1, 3), (0, 2), (1, 0), (0, 1), (0, 3)]
ALL = [(a, b) for b in (2, 1, 3, 0) for a in (0, 1)]


def dot(a, b):
    return lax.dot_general(a, b, (((1,), (0,)), ((), ())), preferred_element_type=F32)


def dot_t(a, b):
    return lax.dot_general(a, b, (((0,), (0,)), ((), ())), preferred_element_type=F32)


def split(value):
    high = value.astype(BF16)
    return high, (value - high.astype(F32)).astype(BF16)


def kernel(
    k_ref, l_ref, e_ref, y_ref, x_ref,
    stage, mh, ml, part, acc, ops, gf, gb, rf, rb, hold, ksend, kx, yfull, xfull, ybuf, xbuf,
    ld_sem, mate_s, mate_r, free, k_s, k_r, k0_s, k0_r, y_s, y_r, x_s, x_r,
    rs_s, rs_r, ag_s, ag_r, brs_s, brs_r, bag_s, bag_r,
):
    r = lax.axis_index("prow")
    p = lax.axis_index("pcol")
    c = lax.rem(p, 2)
    q = p // 2
    mate = (r, p + 1 - 2 * c)

    def across(row):
        return lax.rem(row + 4, 8)

    turned = across(r)

    def member(me, offset):
        return lax.rem(me // 4 + offset[0], 2) * 4 + lax.rem(lax.rem(me, 4) + offset[1], 4)

    def remote(src, dst, send, recv, device):
        return pltpu.make_async_remote_copy(
            src_ref=src, dst_ref=dst, send_sem=send, recv_sem=recv, device_id=device, device_id_type=MESH
        )

    def several(buf, send, recv, count):
        view = buf.at[pl.ds(0, count)]
        return remote(view, view, send, recv, mate)

    def source(n):
        name, half = TILES[n // 2], n % 2
        if name[0] == "E":
            return e_ref.at[name[1], :, half]
        return l_ref.at[name[1] * (name[1] - 1) // 2 + name[2], :, half]

    def own(n):
        s = n % SLOTS
        return pltpu.make_async_copy(source(n), stage.at[s, c], ld_sem.at[s])

    def shared(n):
        s = n % SLOTS
        return remote(source(n), stage.at[s, c], mate_s.at[s], mate_r.at[s], mate)

    def convert(n):
        s = n % SLOTS
        own(n).wait()
        shared(n).wait()
        for kh in range(2):

            @pl.loop(0, 8)
            def _(a):
                high, low = split(stage[s, kh, a])
                rows = pl.ds(pl.multiple_of(a * 64, 64), 64)
                mh[n // 2, kh, n % 2, rows, :] = high
                ml[n // 2, kh, n % 2, rows, :] = low

        if n + SLOTS < HALVES:
            pl.semaphore_signal(free, inc=1, device_id=mate, device_id_type=MESH)
        following = n - 1 + SLOTS
        if n >= 1 and following < HALVES:
            pl.semaphore_wait(free, 1)
            own(following).start()
            shared(following).start()

    for n in range(SLOTS):
        own(n).start()
    for k in range(4):
        ksend[0, k] = k_ref[k, :, 0:128]
        ksend[1, k] = k_ref[k, :, 128:256]
    gf[0, c, r] = jnp.where(c == 0, k_ref[0, :, 0:128], k_ref[0, :, 128:256])
    for h in range(2):
        rf[0, h] = jnp.zeros((8, 64, 128), F32)
        gb[0, h] = jnp.zeros((8, 64, 128), F32)

    barrier = pltpu.get_barrier_semaphore()

    def greet(device):
        pl.semaphore_signal(barrier, inc=1, device_id=device, device_id_type=MESH)

    greet(mate)
    for offset in FAR_FIRST:
        greet((member(r, offset), p))
        greet((member(r, offset), mate[1]))
        greet((turned, 2 * member(q, offset) + c))
    pl.semaphore_wait(barrier, 22)

    def first(offset, same):
        row = member(r, offset)
        half = c if same else 1 - c
        return remote(
            ksend.at[half, 0], gf.at[0, c, r], k0_s.at[0 if same else 1], k0_r.at[0 if same else 1],
            (row, p if same else mate[1]),
        )

    for offset in FAR_FIRST:
        first(offset, True).start()
        first(offset, False).start()
    first((0, 0), False).start()
    for n in range(SLOTS):
        shared(n).start()

    def later(core):
        return remote(ksend.at[core], kx.at[c], k_s.at[core], k_r.at[c], (turned, 2 * q + core))

    def arrived(core):
        return remote(ksend.at[core], kx.at[core], k_s.at[core], k_r.at[core], mate)

    for core in range(2):
        later(core).start()

    class Forward:
        @staticmethod
        def product(i, kh, oh, b, at):
            rows = pl.ds(at, CHUNK)
            wide = dot(mh[i, kh, oh, rows, :], ops[b, kh])
            return wide[:, 0:128] + wide[:, 128:256] + dot(ml[i, kh, oh, rows, :], ops[b, kh, :, 0:128])

    class Backward:
        @staticmethod
        def product(i, kh, oh, b, at):
            cols = pl.ds(at, CHUNK)
            wide = dot_t(mh[i, oh, kh, :, cols], ops[b, kh])
            return wide[:, 0:128] + wide[:, 128:256] + dot_t(ml[i, oh, kh, :, cols], ops[b, kh, :, 0:128])

    PER = CHUNK // 64

    def chunks():
        return range(0, 512, CHUNK)

    def groups(value):
        return value.reshape(PER, 64, 128)

    def over_columns(n, needed, message):
        for j, offset in enumerate(ALL):
            other = member(q, offset)
            if n > 0:
                message(j, other)
            else:
                pl.when(needed(other))(lambda j=j, other=other: message(j, other))

    def from_columns(n, needed, message):
        for j, offset in enumerate(ALL):
            other = member(q, (offset[0], (4 - offset[1]) % 4))
            if n > 0:
                message(j, other)
            else:
                pl.when(needed(other))(lambda j=j, other=other: message(j, other))

    def below(other):
        return other >= q

    def above(other):
        return other <= q

    def fwd_gather_start(par, h, value):
        gf[par, h, turned] = value
        for offset in FAR_FIRST:
            remote(
                gf.at[par, h, turned], gf.at[par, h, turned], ag_s.at[par, h], ag_r.at[par, h],
                (member(r, offset), p),
            ).start()

    def fwd_gather_wait(n, h):
        par = min(n, 1)
        several(gf.at[par, h], ag_s.at[par, h], ag_r.at[par, h], 7).wait_recv()

    def fwd_gather_sent(n, h):
        par = min(n, 1)
        several(gf.at[par, h], ag_s.at[par, h], ag_r.at[par, h], 7).wait_send()

    def fwd_message(n, h):
        def make(j, other):
            return remote(
                part.at[min(n, 1), h, other], rf.at[n, h, j], rs_s.at[n, h, j], rs_r.at[n, h, j],
                (turned, 2 * other + c),
            )

        return make

    def fwd_sum_start(n, h, natural):
        over_columns(n, below, lambda j, other: fwd_message(n, h)(j, other).start())

    def fwd_sum_finish(n, h, natural):
        from_columns(n, above, lambda j, other: fwd_message(n, h)(j, other).wait_recv())
        total = rf[n, h, 0]
        for j in range(1, 8):
            total = total + rf[n, h, j]
        return total

    def fwd_sum_sent(n, h):
        over_columns(n, below, lambda j, other: fwd_message(n, h)(j, other).wait_send())

    def bwd_message(n, h):
        def make(j, other):
            return remote(
                hold.at[min(n, 1), h], gb.at[n, h, q], bag_s.at[n, h, j], bag_r.at[n, h, j],
                (turned, 2 * other + c),
            )

        return make

    def bwd_gather_start(n, h, value):
        hold[min(n, 1), h] = value
        over_columns(n, above, lambda j, other: bwd_message(n, h)(j, other).start())

    def bwd_gather_wait(n, h):
        def wait(j, other):
            slot = gb.at[n, h, other]
            remote(slot, slot, bag_s.at[n, h, j], bag_r.at[n, h, j], mate).wait_recv()

        from_columns(n, below, wait)

    def bwd_gather_sent(n, h):
        over_columns(n, above, lambda j, other: bwd_message(n, h)(j, other).wait_send())

    def bwd_sum_start(n, h, natural):
        par = min(n, 1)
        for j, offset in enumerate(FAR_FIRST):
            other = member(r, offset)
            remote(
                part.at[par, h, other if natural else across(other)], rb.at[par, h, j],
                brs_s.at[par, h], brs_r.at[par, h], (other, p),
            ).start()

    def bwd_sum_finish(n, h, natural):
        par = min(n, 1)
        total = part[par, h, r if natural else turned]
        several(rb.at[par, h], brs_s.at[par, h], brs_r.at[par, h], 7).wait_recv()
        for j in range(7):
            total = total + rb[par, h, j]
        return total

    def bwd_sum_sent(n, h):
        par = min(n, 1)
        several(rb.at[par, h], brs_s.at[par, h], brs_r.at[par, h], 7).wait_send()

    Forward.g, Forward.gather_wait, Forward.gather_sent = gf, staticmethod(fwd_gather_wait), staticmethod(fwd_gather_sent)
    Forward.sum_start, Forward.sum_finish = staticmethod(fwd_sum_start), staticmethod(fwd_sum_finish)
    Forward.sum_sent = staticmethod(fwd_sum_sent)
    Backward.g, Backward.gather_wait, Backward.gather_sent = gb, staticmethod(bwd_gather_wait), staticmethod(bwd_gather_sent)
    Backward.sum_start, Backward.sum_finish = staticmethod(bwd_sum_start), staticmethod(bwd_sum_finish)
    Backward.sum_sent = staticmethod(bwd_sum_sent)

    def take(way, n, h, b):
        high, low = split(way.g[n if way is Backward else min(n, 1), h].reshape(512, 128))
        ops[b, h, :, 0:128] = high
        ops[b, h, :, 128:256] = low

    def aside(way, i, b, slot, first):
        def run(oh):
            for at in chunks():
                out = way.product(i, 0, oh, b, at) + way.product(i, 1, oh, b, at)
                where = pl.ds(at // 64, PER)
                out = groups(out)
                acc[slot, oh, where] = out if first else acc[slot, oh, where] + out

        return [lambda oh=oh: run(oh) for oh in range(2)]

    def step(way, n, i, b, slot, after, summing, gathering, opening=False, natural=False):
        par = min(n, 1)
        if not opening:
            way.gather_wait(n, 0)
        take(way, n, 0, b)
        for oh in range(2):
            for at in chunks():
                where = pl.ds(at // 64, PER)
                out = groups(way.product(i, 0, oh, b, at))
                part[par, oh, where] = out if slot is None else out + acc[slot, oh, where]
        if not opening:
            way.gather_wait(n, 1)
        take(way, n, 1, b)
        for oh in range(2):
            for at in chunks():
                where = pl.ds(at // 64, PER)
                part[par, oh, where] = part[par, oh, where] + groups(way.product(i, 1, oh, b, at))
            way.sum_start(n, oh, natural)
        if not opening:
            for h in range(2):
                way.gather_sent(n, h)
        for run in summing:
            run()
        for h in range(2):
            after(h, way.sum_finish(n, h, natural))
        for run in gathering:
            run()
        for h in range(2):
            way.sum_sent(n, h)

    def hand_over(full, buf, k, sems, pp):
        return remote(
            full.at[k, pp], buf.at[k, c], sems[0].at[k, pp], sems[1].at[k, c], (turned, 2 * q + pp)
        )

    def handed_over(full, buf, k, sems, core):
        remote(full.at[k, core], buf.at[k, core], sems[0].at[k, core], sems[1].at[k, core], mate).wait()

    def conv(*names):
        return [lambda n=n: convert(n) for name in names for n in (2 * TILE[name], 2 * TILE[name] + 1)]

    for run in conv(("E", 0)):
        run()
    several(gf.at[0, c], k0_s.at[0], k0_r.at[0], 7).wait()
    several(gf.at[0, 1 - c], k0_s.at[1], k0_r.at[1], 8).wait()
    fill = {
        ("E", 0): (conv(("L", 1, 0)), conv(("E", 1))),
        ("L", 0): (conv(("L", 2, 1)), conv(("L", 2, 0))),
        ("E", 1): (aside(Forward, TILE["L", 2, 0], 1, 0, True), conv(("L", 3, 0))),
        ("L", 1): (conv(("E", 2)), aside(Forward, TILE["L", 3, 0], 1, 1, True) + conv(("L", 3, 2))),
        ("E", 2): (conv(("L", 3, 1)), aside(Forward, TILE["L", 3, 1], 2, 1, False)),
        ("L", 2): (conv(("E", 3)), []),
        ("E", 3): ([], []),
    }
    for k in range(4):
        last = k == 3

        def solved(h, value, k=k, last=last):
            yfull[k, h] = value
            if last:
                bwd_gather_start(0, h, value)
            else:
                fwd_gather_start(1, h, value)

        step(Forward, 0, TILE["E", k], 0, None, solved, *fill["E", k], opening=k == 0)
        for pp in range(2):
            hand_over(yfull, ybuf, k, (y_s, y_r), pp).start()
        if not last:
            if k == 0:
                for core in range(2):
                    arrived(core).wait()

            def reduced(h, value, k=k):
                fwd_gather_start(0, h, kx[h, k + 1] - value)

            slot = None if k == 0 else k - 1
            step(Forward, 1 + k, TILE["L", k + 1, k], 1 + k, slot, reduced, *fill["L", k])

    fill = {
        ("E", 3): ([], []),
        ("L", 3): (aside(Backward, TILE["L", 3, 1], 1, 1, True), aside(Backward, TILE["L", 3, 0], 1, 0, True)),
        ("E", 2): ([], []),
        ("L", 2): (aside(Backward, TILE["L", 2, 0], 2, 0, False), []),
        ("E", 1): ([], []),
        ("L", 1): ([], []),
        ("E", 0): ([], []),
    }
    for k in range(3, -1, -1):

        def solved(h, value, k=k):
            xfull[k, h] = value
            if k > 0:
                bwd_gather_start(4 - k, h, value)

        step(Backward, 0, TILE["E", k], 0, None, solved, *fill["E", k], natural=k == 0)
        if k > 0:
            for pp in range(2):
                hand_over(xfull, xbuf, k, (x_s, x_r), pp).start()

            def reduced(h, value, k=k):
                bwd_gather_start(0, h, yfull[k - 1, h] - value)

            slot = None if k == 3 else k - 1
            step(Backward, 4 - k, TILE["L", k, k - 1], 4 - k, slot, reduced, *fill["L", k])

    final = remote(xfull.at[0, 1 - c], xbuf.at[0, c], x_s.at[0, 0], x_r.at[0, 0], mate)
    final.start()
    xbuf[0, c] = xfull[0, c]
    for k in range(4):
        for core in range(2):
            handed_over(yfull, ybuf, k, (y_s, y_r), core)
            y_ref[k, :, 128 * core : 128 * core + 128] = ybuf[k, core]
    for k in range(3, -1, -1):
        if k == 0:
            final.wait()
        for core in range(2):
            if k > 0:
                handed_over(xfull, xbuf, k, (x_s, x_r), core)
            x_ref[k, :, 128 * core : 128 * core + 128] = xbuf[k, core]


def local(k_star, lower_blocks, diag_inverse):
    steps, _, piece, cols = k_star.shape
    pairs, segments, _, width = lower_blocks.shape
    dma = pltpu.SemaphoreType.DMA
    n = len(TILES)
    pieces = pltpu.VMEM((steps, 2, piece, cols // 2), F32)
    halves = pltpu.VMEM((2, steps, piece, cols // 2), F32)
    slots = pltpu.VMEM((2, 2, 8, piece, cols // 2), F32)
    more = pltpu.VMEM((4, 2, 8, piece, cols // 2), F32)
    y, x = pl.pallas_call(
        kernel,
        out_shape=[jax.ShapeDtypeStruct((steps, piece, cols), F32)] * 2,
        in_specs=[
            pl.BlockSpec(memory_space=pltpu.VMEM),
            pl.BlockSpec(memory_space=pl.ANY),
            pl.BlockSpec(memory_space=pl.ANY),
        ],
        out_specs=[pl.BlockSpec(memory_space=pltpu.VMEM)] * 2,
        scratch_shapes=[
            pltpu.VMEM((SLOTS, 2, 8, piece, width), F32),
            pltpu.VMEM((n, 2, 2, 512, width), BF16),
            pltpu.VMEM((n, 2, 2, 512, width), BF16),
            slots,
            slots,
            pltpu.VMEM((4, 2, 512, 256), BF16),
            slots, more,
            more, slots,
            pltpu.VMEM((2, 2, piece, cols // 2), F32),
            halves, halves,
            pieces, pieces, pieces, pieces,
            dma((SLOTS,)), dma((SLOTS,)), dma((SLOTS,)),
            pltpu.SemaphoreType.REGULAR,
            dma((2,)), dma((2,)), dma((2,)), dma((2,)),
            dma((4, 2)), dma((4, 2)), dma((4, 2)), dma((4, 2)),
            dma((4, 2, 8)), dma((4, 2, 8)),
            dma((2, 2)), dma((2, 2)),
            dma((2, 2)), dma((2, 2)),
            dma((4, 2, 8)), dma((4, 2, 8)),
        ],
        compiler_params=pltpu.CompilerParams(
            collective_id=0, has_side_effects=True, vmem_limit_bytes=62 * 1024 * 1024
        ),
    )(
        k_star.reshape(steps, piece, cols),
        lower_blocks.reshape(pairs, segments // 2, 2, piece, width),
        diag_inverse.reshape(steps, segments // 2, 2, piece, width),
    )

    shape = (steps, 1, piece, cols)
    return y.reshape(shape), x.reshape(shape)


def solution(mesh):
    return jax.shard_map(
        local,
        mesh=mesh,
        in_specs=(
            P(None, "pcol", "prow", None),
            P(None, None, "prow", "pcol"),
            P(None, None, "prow", "pcol"),
        ),
        out_specs=(P(None, "pcol", "prow", None), P(None, "pcol", "prow", None)),
        check_vma=False,
    )
```

```python
import jax
import jax.numpy as jnp
from jax import lax
from jax.experimental import pallas as pl
from jax.experimental.pallas import tpu as pltpu
from jax.sharding import PartitionSpec as P

MESH = pl.DeviceIdType.MESH
F32 = jnp.float32
BF16 = jnp.bfloat16

SLOTS = 4
CHUNK = 512
TILES = [
    ("E", 0), ("L", 1, 0), ("E", 1), ("L", 2, 1), ("L", 2, 0),
    ("L", 3, 0), ("E", 2), ("L", 3, 2), ("L", 3, 1), ("E", 3),
]
TILE = {name: index for index, name in enumerate(TILES)}
HALVES = 2 * len(TILES)
FAR_FIRST = [(1, 2), (1, 1), (1, 3), (0, 2), (1, 0), (0, 1), (0, 3)]
ALL = [(a, b) for b in (2, 1, 3, 0) for a in (0, 1)]


def dot(a, b):
    return lax.dot_general(a, b, (((1,), (0,)), ((), ())), preferred_element_type=F32)


def dot_t(a, b):
    return lax.dot_general(a, b, (((0,), (0,)), ((), ())), preferred_element_type=F32)


def split(value):
    high = value.astype(BF16)
    return high, (value - high.astype(F32)).astype(BF16)


def kernel(
    k_ref, l_ref, e_ref, y_ref, x_ref,
    stage, mh, ml, part, acc, ops, gf, gb, rf, rb, hold, ksend, kx, yfull, xfull, ybuf, xbuf,
    ld_sem, mate_s, mate_r, free, k_s, k_r, k0_s, k0_r, y_s, y_r, x_s, x_r,
    rs_s, rs_r, ag_s, ag_r, brs_s, brs_r, bag_s, bag_r,
):
    r = lax.axis_index("prow")
    p = lax.axis_index("pcol")
    c = lax.rem(p, 2)
    q = p // 2
    mate = (r, p + 1 - 2 * c)

    def across(row):
        return lax.rem(row + 4, 8)

    turned = across(r)

    def member(me, offset):
        return lax.rem(me // 4 + offset[0], 2) * 4 + lax.rem(lax.rem(me, 4) + offset[1] * (1 + 2 * c), 4)

    def remote(src, dst, send, recv, device):
        return pltpu.make_async_remote_copy(
            src_ref=src, dst_ref=dst, send_sem=send, recv_sem=recv, device_id=device, device_id_type=MESH
        )

    def several(buf, send, recv, count):
        view = buf.at[pl.ds(0, count)]
        return remote(view, view, send, recv, mate)

    def source(n):
        name, half = TILES[n // 2], n % 2
        if name[0] == "E":
            return e_ref.at[name[1], :, half]
        return l_ref.at[name[1] * (name[1] - 1) // 2 + name[2], :, half]

    def own(n):
        s = n % SLOTS
        return pltpu.make_async_copy(source(n), stage.at[s, c], ld_sem.at[s])

    def shared(n):
        s = n % SLOTS
        return remote(source(n), stage.at[s, c], mate_s.at[s], mate_r.at[s], mate)

    def convert(n):
        s = n % SLOTS
        own(n).wait()
        shared(n).wait()
        for kh in range(2):

            @pl.loop(0, 8)
            def _(a):
                high, low = split(stage[s, kh, a])
                rows = pl.ds(pl.multiple_of(a * 64, 64), 64)
                mh[n // 2, kh, n % 2, rows, :] = high
                ml[n // 2, kh, n % 2, rows, :] = low

        if n + SLOTS < HALVES:
            pl.semaphore_signal(free, inc=1, device_id=mate, device_id_type=MESH)
        following = n - 1 + SLOTS
        if n >= 1 and following < HALVES:
            pl.semaphore_wait(free, 1)
            own(following).start()
            shared(following).start()

    for n in range(SLOTS):
        own(n).start()
    for k in range(4):
        ksend[0, k] = k_ref[k, :, 0:128]
        ksend[1, k] = k_ref[k, :, 128:256]
    gf[0, c, r] = jnp.where(c == 0, k_ref[0, :, 0:128], k_ref[0, :, 128:256])
    for h in range(2):
        rf[0, h] = jnp.zeros((8, 64, 128), F32)
        gb[0, h] = jnp.zeros((8, 64, 128), F32)

    barrier = pltpu.get_barrier_semaphore()

    def greet(device):
        pl.semaphore_signal(barrier, inc=1, device_id=device, device_id_type=MESH)

    greet(mate)
    for offset in FAR_FIRST:
        greet((member(r, offset), p))
        greet((member(r, offset), mate[1]))
        greet((turned, 2 * member(q, offset) + c))
    pl.semaphore_wait(barrier, 22)

    def first(offset, same):
        row = member(r, offset)
        half = c if same else 1 - c
        return remote(
            ksend.at[half, 0], gf.at[0, c, r], k0_s.at[0 if same else 1], k0_r.at[0 if same else 1],
            (row, p if same else mate[1]),
        )

    for offset in FAR_FIRST:
        first(offset, True).start()
        first(offset, False).start()
    first((0, 0), False).start()
    for n in range(SLOTS):
        shared(n).start()

    def later(core):
        return remote(ksend.at[core], kx.at[c], k_s.at[core], k_r.at[c], (turned, 2 * q + core))

    def arrived(core):
        return remote(ksend.at[core], kx.at[core], k_s.at[core], k_r.at[core], mate)

    for core in range(2):
        later(core).start()

    class Forward:
        @staticmethod
        def product(i, kh, oh, b, at):
            rows = pl.ds(at, CHUNK)
            wide = dot(mh[i, kh, oh, rows, :], ops[b, kh])
            return wide[:, 0:128] + wide[:, 128:256] + dot(ml[i, kh, oh, rows, :], ops[b, kh, :, 0:128])

    class Backward:
        @staticmethod
        def product(i, kh, oh, b, at):
            cols = pl.ds(at, CHUNK)
            wide = dot_t(mh[i, oh, kh, :, cols], ops[b, kh])
            return wide[:, 0:128] + wide[:, 128:256] + dot_t(ml[i, oh, kh, :, cols], ops[b, kh, :, 0:128])

    PER = CHUNK // 64

    def chunks():
        return range(0, 512, CHUNK)

    def groups(value):
        return value.reshape(PER, 64, 128)

    def over_columns(n, needed, message):
        for j, offset in enumerate(ALL):
            other = member(q, offset)
            if n > 0:
                message(j, other)
            else:
                pl.when(needed(other))(lambda j=j, other=other: message(j, other))

    def from_columns(n, needed, message):
        for j, offset in enumerate(ALL):
            other = member(q, (offset[0], (4 - offset[1]) % 4))
            if n > 0:
                message(j, other)
            else:
                pl.when(needed(other))(lambda j=j, other=other: message(j, other))

    def below(other):
        return other >= q

    def above(other):
        return other <= q

    def fwd_gather_start(par, h, value):
        gf[par, h, turned] = value
        for offset in FAR_FIRST:
            remote(
                gf.at[par, h, turned], gf.at[par, h, turned], ag_s.at[par, h], ag_r.at[par, h],
                (member(r, offset), p),
            ).start()

    def fwd_gather_wait(n, h):
        par = min(n, 1)
        several(gf.at[par, h], ag_s.at[par, h], ag_r.at[par, h], 7).wait_recv()

    def fwd_gather_sent(n, h):
        par = min(n, 1)
        several(gf.at[par, h], ag_s.at[par, h], ag_r.at[par, h], 7).wait_send()

    def fwd_message(n, h):
        def make(j, other):
            return remote(
                part.at[min(n, 1), h, other], rf.at[n, h, j], rs_s.at[n, h, j], rs_r.at[n, h, j],
                (turned, 2 * other + c),
            )

        return make

    def fwd_sum_start(n, h, natural):
        over_columns(n, below, lambda j, other: fwd_message(n, h)(j, other).start())

    def fwd_sum_finish(n, h, natural):
        from_columns(n, above, lambda j, other: fwd_message(n, h)(j, other).wait_recv())
        total = rf[n, h, 0]
        for j in range(1, 8):
            total = total + rf[n, h, j]
        return total

    def fwd_sum_sent(n, h):
        over_columns(n, below, lambda j, other: fwd_message(n, h)(j, other).wait_send())

    def bwd_message(n, h):
        def make(j, other):
            return remote(
                hold.at[min(n, 1), h], gb.at[n, h, q], bag_s.at[n, h, j], bag_r.at[n, h, j],
                (turned, 2 * other + c),
            )

        return make

    def bwd_gather_start(n, h, value):
        hold[min(n, 1), h] = value
        over_columns(n, above, lambda j, other: bwd_message(n, h)(j, other).start())

    def bwd_gather_wait(n, h):
        def wait(j, other):
            slot = gb.at[n, h, other]
            remote(slot, slot, bag_s.at[n, h, j], bag_r.at[n, h, j], mate).wait_recv()

        from_columns(n, below, wait)

    def bwd_gather_sent(n, h):
        over_columns(n, above, lambda j, other: bwd_message(n, h)(j, other).wait_send())

    def bwd_sum_start(n, h, natural):
        par = min(n, 1)
        for j, offset in enumerate(FAR_FIRST):
            other = member(r, offset)
            remote(
                part.at[par, h, other if natural else across(other)], rb.at[par, h, j],
                brs_s.at[par, h], brs_r.at[par, h], (other, p),
            ).start()

    def bwd_sum_finish(n, h, natural):
        par = min(n, 1)
        total = part[par, h, r if natural else turned]
        several(rb.at[par, h], brs_s.at[par, h], brs_r.at[par, h], 7).wait_recv()
        for j in range(7):
            total = total + rb[par, h, j]
        return total

    def bwd_sum_sent(n, h):
        par = min(n, 1)
        several(rb.at[par, h], brs_s.at[par, h], brs_r.at[par, h], 7).wait_send()

    Forward.g, Forward.gather_wait, Forward.gather_sent = gf, staticmethod(fwd_gather_wait), staticmethod(fwd_gather_sent)
    Forward.sum_start, Forward.sum_finish = staticmethod(fwd_sum_start), staticmethod(fwd_sum_finish)
    Forward.sum_sent = staticmethod(fwd_sum_sent)
    Backward.g, Backward.gather_wait, Backward.gather_sent = gb, staticmethod(bwd_gather_wait), staticmethod(bwd_gather_sent)
    Backward.sum_start, Backward.sum_finish = staticmethod(bwd_sum_start), staticmethod(bwd_sum_finish)
    Backward.sum_sent = staticmethod(bwd_sum_sent)

    def take(way, n, h, b):
        high, low = split(way.g[n if way is Backward else min(n, 1), h].reshape(512, 128))
        ops[b, h, :, 0:128] = high
        ops[b, h, :, 128:256] = low

    def aside(way, i, b, slot, first):
        def run(oh):
            for at in chunks():
                out = way.product(i, 0, oh, b, at) + way.product(i, 1, oh, b, at)
                where = pl.ds(at // 64, PER)
                out = groups(out)
                acc[slot, oh, where] = out if first else acc[slot, oh, where] + out

        return [lambda oh=oh: run(oh) for oh in range(2)]

    def step(way, n, i, b, slot, after, summing, gathering, opening=False, natural=False):
        par = min(n, 1)
        if not opening:
            way.gather_wait(n, 0)
        take(way, n, 0, b)
        for oh in range(2):
            for at in chunks():
                where = pl.ds(at // 64, PER)
                out = groups(way.product(i, 0, oh, b, at))
                part[par, oh, where] = out if slot is None else out + acc[slot, oh, where]
        if not opening:
            way.gather_wait(n, 1)
        take(way, n, 1, b)
        for oh in range(2):
            for at in chunks():
                where = pl.ds(at // 64, PER)
                part[par, oh, where] = part[par, oh, where] + groups(way.product(i, 1, oh, b, at))
            way.sum_start(n, oh, natural)
        if not opening:
            for h in range(2):
                way.gather_sent(n, h)
        for run in summing:
            run()
        for h in range(2):
            after(h, way.sum_finish(n, h, natural))
        for run in gathering:
            run()
        for h in range(2):
            way.sum_sent(n, h)

    def hand_over(full, buf, k, sems, pp):
        return remote(
            full.at[k, pp], buf.at[k, c], sems[0].at[k, pp], sems[1].at[k, c], (turned, 2 * q + pp)
        )

    def handed_over(full, buf, k, sems, core):
        remote(full.at[k, core], buf.at[k, core], sems[0].at[k, core], sems[1].at[k, core], mate).wait()

    def conv(*names):
        return [lambda n=n: convert(n) for name in names for n in (2 * TILE[name], 2 * TILE[name] + 1)]

    for run in conv(("E", 0)):
        run()
    several(gf.at[0, c], k0_s.at[0], k0_r.at[0], 7).wait()
    several(gf.at[0, 1 - c], k0_s.at[1], k0_r.at[1], 8).wait()
    fill = {
        ("E", 0): (conv(("L", 1, 0)), conv(("E", 1))),
        ("L", 0): (conv(("L", 2, 1)), conv(("L", 2, 0))),
        ("E", 1): (aside(Forward, TILE["L", 2, 0], 1, 0, True), conv(("L", 3, 0))),
        ("L", 1): (conv(("E", 2)), aside(Forward, TILE["L", 3, 0], 1, 1, True) + conv(("L", 3, 2))),
        ("E", 2): (conv(("L", 3, 1)), aside(Forward, TILE["L", 3, 1], 2, 1, False)),
        ("L", 2): (conv(("E", 3)), []),
        ("E", 3): ([], []),
    }
    for k in range(4):
        last = k == 3

        def solved(h, value, k=k, last=last):
            yfull[k, h] = value
            if last:
                bwd_gather_start(0, h, value)
            else:
                fwd_gather_start(1, h, value)

        step(Forward, 0, TILE["E", k], 0, None, solved, *fill["E", k], opening=k == 0)
        for pp in range(2):
            hand_over(yfull, ybuf, k, (y_s, y_r), pp).start()
        if not last:
            if k == 0:
                for core in range(2):
                    arrived(core).wait()

            def reduced(h, value, k=k):
                fwd_gather_start(0, h, kx[h, k + 1] - value)

            slot = None if k == 0 else k - 1
            step(Forward, 1 + k, TILE["L", k + 1, k], 1 + k, slot, reduced, *fill["L", k])

    fill = {
        ("E", 3): ([], []),
        ("L", 3): (aside(Backward, TILE["L", 3, 1], 1, 1, True), aside(Backward, TILE["L", 3, 0], 1, 0, True)),
        ("E", 2): ([], []),
        ("L", 2): (aside(Backward, TILE["L", 2, 0], 2, 0, False), []),
        ("E", 1): ([], []),
        ("L", 1): ([], []),
        ("E", 0): ([], []),
    }
    for k in range(3, -1, -1):

        def solved(h, value, k=k):
            xfull[k, h] = value
            if k > 0:
                bwd_gather_start(4 - k, h, value)

        step(Backward, 0, TILE["E", k], 0, None, solved, *fill["E", k], natural=k == 0)
        if k > 0:
            for pp in range(2):
                hand_over(xfull, xbuf, k, (x_s, x_r), pp).start()

            def reduced(h, value, k=k):
                bwd_gather_start(0, h, yfull[k - 1, h] - value)

            slot = None if k == 3 else k - 1
            step(Backward, 4 - k, TILE["L", k, k - 1], 4 - k, slot, reduced, *fill["L", k])

    final = remote(xfull.at[0, 1 - c], xbuf.at[0, c], x_s.at[0, 0], x_r.at[0, 0], mate)
    final.start()
    xbuf[0, c] = xfull[0, c]
    for k in range(4):
        for core in range(2):
            handed_over(yfull, ybuf, k, (y_s, y_r), core)
            y_ref[k, :, 128 * core : 128 * core + 128] = ybuf[k, core]
    for k in range(3, -1, -1):
        if k == 0:
            final.wait()
        for core in range(2):
            if k > 0:
                handed_over(xfull, xbuf, k, (x_s, x_r), core)
            x_ref[k, :, 128 * core : 128 * core + 128] = xbuf[k, core]


def local(k_star, lower_blocks, diag_inverse):
    steps, _, piece, cols = k_star.shape
    pairs, segments, _, width = lower_blocks.shape
    dma = pltpu.SemaphoreType.DMA
    n = len(TILES)
    pieces = pltpu.VMEM((steps, 2, piece, cols // 2), F32)
    halves = pltpu.VMEM((2, steps, piece, cols // 2), F32)
    slots = pltpu.VMEM((2, 2, 8, piece, cols // 2), F32)
    more = pltpu.VMEM((4, 2, 8, piece, cols // 2), F32)
    y, x = pl.pallas_call(
        kernel,
        out_shape=[jax.ShapeDtypeStruct((steps, piece, cols), F32)] * 2,
        in_specs=[
            pl.BlockSpec(memory_space=pltpu.VMEM),
            pl.BlockSpec(memory_space=pl.ANY),
            pl.BlockSpec(memory_space=pl.ANY),
        ],
        out_specs=[pl.BlockSpec(memory_space=pltpu.VMEM)] * 2,
        scratch_shapes=[
            pltpu.VMEM((SLOTS, 2, 8, piece, width), F32),
            pltpu.VMEM((n, 2, 2, 512, width), BF16),
            pltpu.VMEM((n, 2, 2, 512, width), BF16),
            slots,
            slots,
            pltpu.VMEM((4, 2, 512, 256), BF16),
            slots, more,
            more, slots,
            pltpu.VMEM((2, 2, piece, cols // 2), F32),
            halves, halves,
            pieces, pieces, pieces, pieces,
            dma((SLOTS,)), dma((SLOTS,)), dma((SLOTS,)),
            pltpu.SemaphoreType.REGULAR,
            dma((2,)), dma((2,)), dma((2,)), dma((2,)),
            dma((4, 2)), dma((4, 2)), dma((4, 2)), dma((4, 2)),
            dma((4, 2, 8)), dma((4, 2, 8)),
            dma((2, 2)), dma((2, 2)),
            dma((2, 2)), dma((2, 2)),
            dma((4, 2, 8)), dma((4, 2, 8)),
        ],
        compiler_params=pltpu.CompilerParams(
            collective_id=0, has_side_effects=True, vmem_limit_bytes=62 * 1024 * 1024
        ),
    )(
        k_star.reshape(steps, piece, cols),
        lower_blocks.reshape(pairs, segments // 2, 2, piece, width),
        diag_inverse.reshape(steps, segments // 2, 2, piece, width),
    )

    shape = (steps, 1, piece, cols)
    return y.reshape(shape), x.reshape(shape)


def solution(mesh):
    return jax.shard_map(
        local,
        mesh=mesh,
        in_specs=(
            P(None, "pcol", "prow", None),
            P(None, None, "prow", "pcol"),
            P(None, None, "prow", "pcol"),
        ),
        out_specs=(P(None, "pcol", "prow", None), P(None, "pcol", "prow", None)),
        check_vma=False,
    )
```
